128 devices in a mesh: gx: 4 (over x), gy: 4 (over y), gz: 8 (over z, core).
Axes of the slice: x: 4, y: 4, z: 4, core: 2. Of those that a mesh axis runs over, the one named last changes fastest.
Arguments:
- functions: bfloat16 [10240, 8, 4096], P(('gx', 'gy', 'gz')), may hold values from -6 to 6
- responses: bfloat16 [10240, 8, 4096], P(('gx', 'gy', 'gz')), may hold values from -6 to 6
- box_domain: int32 [10240, 1], P(('gx', 'gy', 'gz')), may hold values from 0 to 127, as said below
- pair_index: int32 [2, 10240, 24], P(None, ('gx', 'gy', 'gz')), may hold values from 0 to 7
- pair_weight: float32 [10240, 24], P(('gx', 'gy', 'gz')), may hold values from -6 to 6
- kernel_xc: float32 [128, 8192], P(('gx', 'gy', 'gz')), may hold values from 0.25 to 2
Outputs:
- applied: bfloat16 [10240, 8, 4096], P(('gx', 'gy', 'gz'))
- potential: bfloat16 [128, 8192], P(('gx', 'gy', 'gz'))
The draws below stay inside these ranges and needn't reach their ends.
Inputs may be any that keep to these rules, and one draw needn't show every extreme that they name: `box_domain`: boxes are held near their grid in y and z: a box of the device with mesh coordinates (ix, iy, iz) names domain ((ix + dx) mod 4, (iy + dy) mod 4, (iz + dz) mod 8) with dx in -2, -1, 0, dy in -1, 0 and dz in -1, 0, 1, and every device's boxes use all eighteen such offsets.
All inputs are finite; a program needn't handle non-finite values.
Results may differ from the reference program's by a relative error of at most 0.017.
Values may be sent and summed in bfloat16 or wider, within the bound.
No kernel may reach another device: no remote copies, remote signals or barrier semaphores. Data moves between devices by JAX's collectives and lax.ppermute only.
A program may use at most 128 MiB of HBM per device.

```python
import math
import jax
import jax.numpy as jnp
from jax import lax

CB = 64
FB = 128
NFUN = 8
PAIRS = 24
BOX_DEV = 80
BOXES = 10240
N_GX = 4
N_GY = 4
N_GZ = 8
DEVICES = 128


def draw_box_domain(key, part):
    rows = jnp.arange(BOXES, dtype=jnp.int32)
    owner = rows // BOX_DEV
    within = rows % BOX_DEV
    key_codes = jax.random.fold_in(key, 11)
    key_shift = jax.random.fold_in(key, 23)
    codes = jax.random.randint(key_codes, (BOXES,), 0, 18, dtype=jnp.int32)
    shifts = jax.random.randint(key_shift, (DEVICES,), 0, 18, dtype=jnp.int32)
    first = (within + shifts[owner]) % 18
    codes = jnp.where(within < 18, first, codes)
    delta_x = codes // 6 - 2
    delta_y = codes // 3 % 2 - 1
    delta_z = codes % 3 - 1
    own_x = owner // (N_GY * N_GZ)
    own_y = owner // N_GZ % N_GY
    own_z = owner % N_GZ
    domain = ((own_x + delta_x) % N_GX * N_GY + (own_y + delta_y) % N_GY) * N_GZ + (own_z + delta_z) % N_GZ
    return domain[:, None].astype(jnp.int32)


def set_ends(values, own_key, low, largest):
    longest = values.shape.index(max(values.shape))
    spots = []
    for shift in (0, 1):
        where = [jax.random.randint(jax.random.fold_in(own_key, axis), (), 0, length) for axis, length in enumerate(values.shape)]
        where[longest] = (where[longest] + shift) % values.shape[longest]
        spots.append(tuple(where))
    return values.at[spots[0]].set(low).at[spots[1]].set(largest)


def level_of(stream_key, shape, cuts, smallest, high):
    factor_of, own = 1.0, jax.random.fold_in(stream_key, 6)
    for axis_at, parts in cuts:
        draws = jnp.exp(jax.random.uniform(jax.random.fold_in(own, axis_at), (parts,), jnp.float32, smallest / len(cuts), high / len(cuts)))
        factor_of = factor_of * jnp.repeat(draws, shape[axis_at] // parts).reshape([-1 if axis == axis_at else 1 for axis in range(len(shape))])
    return factor_of


def bell_draw(stream_key, dims, deviation, limit, pieces=(), held_as=jnp.bfloat16):
    loudness = level_of(stream_key, dims, pieces, -0.22, 0.18) if pieces else 1.0
    values = jax.random.normal(stream_key, dims, jnp.float32) * deviation * loudness
    return jnp.minimum(jnp.maximum(values, -limit), limit).astype(held_as)


def setup_inputs(seed: int = 0) -> dict:
    key_of = jax.random.split(jax.random.key(seed), 7)
    return {
        "functions": bell_draw(key_of[0], (BOXES, NFUN, CB * CB), 1.0, 6.0, ((0, 128),)),
        "responses": bell_draw(key_of[1], (BOXES, NFUN, CB * CB), 1.0, 6.0, ((0, 128),)),
        "box_domain": draw_box_domain(jax.random.fold_in(key_of[6], 71), 0),
        "pair_index": set_ends(jax.random.randint(key_of[3], (2, BOXES, PAIRS), 0, NFUN), jax.random.fold_in(key_of[3], 1), 0, NFUN - 1).astype(jnp.int32),
        "pair_weight": bell_draw(key_of[4], (BOXES, PAIRS), 0.4, 6.0, ((0, 128),), jnp.float32),
        "kernel_xc": jnp.clip(jnp.exp(math.log(2.0) - 2.0794415 * jax.random.uniform(key_of[5], (DEVICES, CB * FB), jnp.float32) ** level_of(key_of[5], (DEVICES, CB * FB), ((0, 128),), -0.2, 0.2)), 0.25, 2.0),
    }


HIGH = lax.Precision.HIGHEST


def interp_table(coarse):
    fine_len = 2 * coarse
    fine_pos = jnp.arange(fine_len, dtype=jnp.float32)[:, None]
    coarse_pos = jnp.arange(coarse, dtype=jnp.float32)[None, :]
    frequency = jnp.arange(1, coarse // 2, dtype=jnp.float32)[:, None, None]
    phases = 2.0 * jnp.pi * frequency * (fine_pos / fine_len - coarse_pos / coarse)
    summed = 1.0 + 2.0 * jnp.sum(jnp.cos(phases), axis=0) + jnp.cos(jnp.pi * coarse_pos) * jnp.cos(jnp.pi * fine_pos * coarse / fine_len)
    return (summed / coarse).astype(jnp.bfloat16)


def half_targets(domains, size_x, size_y, size_z):
    index_x = domains // (size_y * size_z)
    index_y = (domains // size_z) % size_y
    index_z = domains % size_z
    shift_x = jnp.array([0, 1], dtype=jnp.int32)
    return ((((index_x[:, None] + shift_x[None, :]) % size_x) * size_y + index_y[:, None]) * size_z + index_z[:, None]).astype(jnp.int32)


def interpolate(planes, table_full):
    box_count, fun_count = planes.shape[0], planes.shape[1]
    shaped = planes.reshape(box_count, fun_count, CB, CB).astype(jnp.float32)
    table = table_full.astype(jnp.float32)
    stretched = jnp.einsum('bfxy,Xx->bfyX', shaped, table, precision=HIGH).astype(jnp.bfloat16)
    return jnp.einsum('bfyX,Yy->bfXY', stretched.astype(jnp.float32), table, precision=HIGH).astype(jnp.bfloat16)


def block_density(func_blk, resp_blk, pidx_blk, weight_blk, table_full):
    fine_f = interpolate(func_blk, table_full)
    fine_r = interpolate(resp_blk, table_full)
    levels = jnp.arange(NFUN, dtype=jnp.int32)
    first_hot = (pidx_blk[0][..., None] == levels).astype(jnp.float32)
    second_hot = (pidx_blk[1][..., None] == levels).astype(jnp.float32)
    kernel_pairs = jnp.einsum('bp,bpf,bpg->bfg', weight_blk, first_hot, second_hot, precision=HIGH).astype(jnp.bfloat16)
    mixed_resp = jnp.einsum('bfg,bgXY->bfXY', kernel_pairs.astype(jnp.float32), fine_r.astype(jnp.float32), precision=HIGH)
    density = jnp.sum(fine_f.astype(jnp.float32) * mixed_resp, axis=1)
    return density.reshape(density.shape[0], 2, CB * FB)


def block_apply(fine_f, box_pot, table_half):
    table = table_half.astype(jnp.float32)
    weighted = (box_pot[:, None].astype(jnp.float32) * fine_f.astype(jnp.float32)).astype(jnp.bfloat16)
    colwise = jnp.einsum('bfXY,Xx->bfYx', weighted.astype(jnp.float32), table, precision=HIGH).astype(jnp.bfloat16)
    result = jnp.einsum('bfYx,Yy->bfxy', colwise.astype(jnp.float32), table, precision=HIGH).astype(jnp.bfloat16)
    return result.reshape(result.shape[0], result.shape[1], CB * CB)


def reference(functions, responses, box_domain, pair_index, pair_weight, kernel_xc):
    table_full = interp_table(CB)
    table_half = table_full * 0.5
    blocks = BOXES // 16
    targets = half_targets(box_domain[:, 0], N_GX, N_GY, N_GZ)

    def blocked(array):
        return array.reshape((blocks, 16) + array.shape[1:])

    pidx_blocks = pair_index.reshape(2, blocks, 16, PAIRS).transpose(1, 0, 2, 3)

    def deposit_step(accumulated, inputs):
        func_blk, resp_blk, pidx_blk, weight_blk, target_blk = inputs
        halves = block_density(func_blk, resp_blk, pidx_blk, weight_blk, table_full)
        return accumulated.at[target_blk.reshape(-1)].add(halves.reshape(-1, CB * FB)), None

    start = jnp.zeros((DEVICES, CB * FB), jnp.float32)
    accumulated, _ = lax.scan(deposit_step, start, (blocked(functions), blocked(responses), pidx_blocks, blocked(pair_weight), blocked(targets)))
    potential = (kernel_xc * accumulated).astype(jnp.bfloat16)

    def apply_step(inputs):
        func_blk, target_blk = inputs
        fine_f = interpolate(func_blk, table_full)
        box_pot = potential[target_blk].reshape(target_blk.shape[0], FB, FB)
        return block_apply(fine_f, box_pot, table_half)

    applied = lax.map(apply_step, (blocked(functions), blocked(targets))).reshape(BOXES, NFUN, CB * CB)
    return applied, potential
```

```python
import jax
import jax.numpy as jnp
import ml_dtypes
import numpy as np
from jax import lax
from jax.experimental import pallas as pl
from jax.experimental.pallas import tpu as pltpu
from jax.sharding import PartitionSpec as P

AXES = ("gx", "gy", "gz")
GROUP = 8
VMEM_LIMIT = 60 * 1024 * 1024
BF16 = jnp.bfloat16
F32 = jnp.float32


def tables():
    m = (2.0 * np.arange(64) + 1.0)[:, None]
    n = np.arange(64.0)[None, :]
    k = np.arange(1, 32)[:, None, None]
    total = 1.0 + 2.0 * np.cos(2.0 * np.pi * k * (m / 128 - n / 64)).sum(0)
    total = total + np.cos(np.pi * n) * np.cos(np.pi * m / 2)
    odd = (total / 64).astype(ml_dtypes.bfloat16)
    x_of = np.concatenate([np.arange(0, 64, 2), np.arange(1, 64, 2)])
    odd_x = odd[x_of][:, x_of]
    wide = np.zeros((256, 256), ml_dtypes.bfloat16)
    for i in range(4):
        wide[64 * i : 64 * i + 64, 64 * i : 64 * i + 64] = odd.T
    return odd_x, wide


def cell_orders():
    rows = np.zeros((64, 64), np.float32)
    for par in range(2):
        for p in range(2):
            for c in range(16):
                rows[4 * c + 2 * p + par, (par * 2 + p) * 16 + c] = 1
    cols = np.zeros((128, 128), np.float32)
    for par in range(2):
        for y in range(64):
            cols[par * 64 + y, 2 * y + par] = 1
    return rows, cols


def lane_low(shape):
    return lax.broadcasted_iota(jnp.int32, shape, len(shape) - 1) % 128 < 64


def slots_of(at, domain):
    box_x = lax.div(domain, 32)
    slot_y = lax.rem(lax.rem(lax.div(domain, 8), 4) - at[0] + 5, 4)
    slot_z = lax.rem(lax.rem(domain, 8) - at[1] + 9, 8)
    base = (slot_z * 2 + slot_y) * 4
    return base + box_x, base + lax.rem(box_x + 1, 4)


def density_kernel(at, domains, func, resp, pidx, pw, spread, odd_x, wide, part, fine, acc, stage, mixer, rs):
    step = pl.program_id(0)
    rows8 = 8 * GROUP

    @pl.when(step == 0)
    def _():
        acc[...] = jnp.zeros_like(acc)

        def widen(a, precision=None):
            return jnp.dot(a, spread[...], precision=precision, preferred_element_type=F32)

        level = (lax.broadcasted_iota(jnp.int32, (24, 640), 1) % 8).astype(F32)
        one = jnp.ones((24, 640), F32)
        weight = widen(pw[...], lax.Precision.HIGHEST)
        first = jnp.where(widen(pidx[0].astype(F32)) == level, weight, 0.0)
        second = jnp.where(widen(pidx[1].astype(F32)) == level, one, 0.0)
        at_row = lax.broadcasted_iota(jnp.int32, (128, 128), 0) // 8
        at_col = lax.broadcasted_iota(jnp.int32, (128, 128), 1) // 8
        for i in range(5):
            cut = slice(128 * i, 128 * i + 128)
            cross = lax.dot_general(
                first[:, cut],
                second[:, cut],
                (((0,), (0,)), ((), ())),
                precision=lax.Precision.HIGHEST,
                preferred_element_type=F32,
            )
            cross = jnp.where(at_row == at_col, cross, 0.0).astype(BF16)
            for j in range(128 // rows8):
                cut = slice(rows8 * j, rows8 * j + rows8)
                mixer[128 // rows8 * i + j] = cross[cut, cut]

    low = lane_low((32, 128))
    mixed = jnp.dot(mixer[step], resp[...].reshape(rows8, 4096), preferred_element_type=F32)
    for b in range(GROUP):
        for c in range(32):
            stage[0, b, 8 * c : 8 * c + 8, :] = func[b, :, 128 * c : 128 * c + 128].astype(F32)
            stage[1, b, 8 * c : 8 * c + 8, :] = mixed[8 * b : 8 * b + 8, 128 * c : 128 * c + 128]

    def place(which, b):
        return fine.at[b, 0] if which == 0 else rs.at[b]

    for b in range(GROUP):
        for which in range(2):
            to = place(which, b)
            for h in range(4):
                one = stage[which, b, pl.ds(2 * h, 32, stride=8), :]
                two = stage[which, b, pl.ds(2 * h + 1, 32, stride=8), :]
                p0 = jnp.where(low, one, pltpu.roll(two, 64, 1)).astype(BF16)
                p1 = jnp.where(low, pltpu.roll(one, 64, 1), two).astype(BF16)
                row, lane = 128 * (h // 2), 128 * (h % 2)
                to[row : row + 32, lane : lane + 128] = p0
                to[row + 32 : row + 64, lane : lane + 128] = p1
    for b in range(GROUP):
        for which in range(2):
            to = place(which, b)
            for i in range(2):
                even = to[128 * i : 128 * i + 64, :]
                odd = jnp.dot(odd_x[...], even, preferred_element_type=F32)
                to[128 * i + 64 : 128 * i + 128, :] = odd.astype(BF16)
    for b in range(GROUP):
        tall_f = fine[b, 0]
        tall_r = rs[b]
        shift_f = jnp.dot(tall_f, wide[...], preferred_element_type=F32)
        shift_r = jnp.dot(tall_r, wide[...], preferred_element_type=F32)
        fine[b, 1] = shift_f.astype(BF16)
        den_e = tall_f.astype(F32) * tall_r.astype(F32)
        den_o = shift_f * shift_r
        s0, s1 = slots_of(at, domains[step * GROUP + b])
        for par, den in ((0, den_e), (1, den_o)):
            den = den[:128] + den[128:]
            den = den[:, :128] + den[:, 128:]
            for g in range(4):
                acc[s0, par, 16 * g : 16 * g + 16] += den[32 * g : 32 * g + 16]
                acc[s1, par, 16 * g : 16 * g + 16] += den[32 * g + 16 : 32 * g + 32]

    @pl.when(step == pl.num_programs(0) - 1)
    def _():
        lowd = lane_low((64, 128))

        def fold(d, _):
            sums = [acc[d, par] + pltpu.roll(acc[d, par], 64, 1) for par in range(2)]
            part[d] = jnp.where(lowd, sums[0], sums[1]).astype(BF16)
            return 0

        lax.fori_loop(0, 24, fold, 0)


def box_density(at, domains, functions, responses, pair_index, pair_weight):
    boxes = functions.shape[0]
    odd_x, wide = tables()
    steps = boxes // GROUP
    spread = np.repeat(np.eye(boxes, dtype=np.float32), 8, axis=1)
    return pl.pallas_call(
        density_kernel,
        grid_spec=pltpu.PrefetchScalarGridSpec(
            num_scalar_prefetch=2,
            grid=(steps,),
            in_specs=[
                pl.BlockSpec((GROUP, 8, 4096), lambda i, *_: (i, 0, 0)),
                pl.BlockSpec((GROUP, 8, 4096), lambda i, *_: (i, 0, 0)),
                pl.BlockSpec((2, 24, boxes), lambda i, *_: (0, 0, 0)),
                pl.BlockSpec((24, boxes), lambda i, *_: (0, 0)),
                pl.BlockSpec((boxes, 8 * boxes), lambda i, *_: (0, 0)),
                pl.BlockSpec((64, 64), lambda i, *_: (0, 0)),
                pl.BlockSpec((256, 256), lambda i, *_: (0, 0)),
            ],
            out_specs=[
                pl.BlockSpec((24, 64, 128), lambda i, *_: (0, 0, 0)),
                pl.BlockSpec((GROUP, 2, 256, 256), lambda i, *_: (i, 0, 0, 0)),
            ],
            scratch_shapes=[
                pltpu.VMEM((24, 2, 64, 128), F32),
                pltpu.VMEM((2, GROUP, 256, 128), F32),
                pltpu.VMEM((steps, 8 * GROUP, 8 * GROUP), BF16),
                pltpu.VMEM((GROUP, 256, 256), BF16),
            ],
        ),
        out_shape=[
            jax.ShapeDtypeStruct((24, 64, 128), BF16),
            jax.ShapeDtypeStruct((boxes, 2, 256, 256), BF16),
        ],
        compiler_params=pltpu.CompilerParams(vmem_limit_bytes=VMEM_LIMIT),
        cost_estimate=pl.CostEstimate(flops=2 * 10**9, bytes_accessed=32 * 10**6, transcendentals=0),
        name="box_density",
    )(
        at,
        domains,
        functions,
        responses,
        jnp.transpose(pair_index, (0, 2, 1)),
        jnp.transpose(pair_weight, (1, 0)),
        jnp.asarray(spread),
        jnp.asarray(odd_x),
        jnp.asarray(wide),
    )


def apply_kernel(at, domains, pot, fine, odd_xt, wide_t, out, twice, stage, col):
    step = pl.program_id(0)

    @pl.when(step == 0)
    def _():
        lowd = lane_low((64, 128))

        def double(d, _):
            own = pot[d].astype(F32) * 0.25
            other = pltpu.roll(own, 64, 1)
            twice[d, 0] = jnp.where(lowd, own, other).astype(BF16)
            twice[d, 1] = jnp.where(lowd, other, own).astype(BF16)
            return 0

        lax.fori_loop(0, 24, double, 0)

    low = lane_low((32, 128))
    for b in range(GROUP):
        s0, s1 = slots_of(at, domains[step * GROUP + b])
        weighted = []
        for par in range(2):
            pieces = []
            for g in range(4):
                pieces.append(twice[s0, par, 16 * g : 16 * g + 16])
                pieces.append(twice[s1, par, 16 * g : 16 * g + 16])
            level = jnp.concatenate(pieces, axis=0)
            level = jnp.concatenate([level, level], axis=1)
            level = jnp.concatenate([level, level], axis=0)
            weighted.append(level * fine[b, par])
        col[b] = weighted[0].astype(F32) + jnp.dot(weighted[1], wide_t[...], preferred_element_type=F32)
    for b in range(GROUP):
        for i in range(2):
            odd = col[b, 128 * i + 64 : 128 * i + 128].astype(BF16)
            res = col[b, 128 * i : 128 * i + 64] + jnp.dot(odd_xt[...], odd, preferred_element_type=F32)
            for k in range(2):
                p0 = res[:32, 128 * k : 128 * k + 128]
                p1 = res[32:, 128 * k : 128 * k + 128]
                f = 4 * i + 2 * k
                stage[b, pl.ds(f, 32, stride=8), :] = jnp.where(low, p0, pltpu.roll(p1, 64, 1))
                stage[b, pl.ds(f + 1, 32, stride=8), :] = jnp.where(low, pltpu.roll(p0, 64, 1), p1)
    for b in range(GROUP):
        for c in range(32):
            out[b, :, 128 * c : 128 * c + 128] = stage[b, 8 * c : 8 * c + 8, :].astype(BF16)


def box_apply(at, domains, pot, fine):
    boxes = fine.shape[0]
    odd_x, wide = tables()
    steps = boxes // GROUP
    return pl.pallas_call(
        apply_kernel,
        grid_spec=pltpu.PrefetchScalarGridSpec(
            num_scalar_prefetch=2,
            grid=(steps,),
            in_specs=[
                pl.BlockSpec((24, 64, 128), lambda i, *_: (0, 0, 0)),
                pl.BlockSpec((GROUP, 2, 256, 256), lambda i, *_: (i, 0, 0, 0)),
                pl.BlockSpec((64, 64), lambda i, *_: (0, 0)),
                pl.BlockSpec((256, 256), lambda i, *_: (0, 0)),
            ],
            out_specs=pl.BlockSpec((GROUP, 8, 4096), lambda i, *_: (i, 0, 0)),
            scratch_shapes=[
                pltpu.VMEM((24, 2, 64, 128), BF16),
                pltpu.VMEM((GROUP, 256, 128), F32),
                pltpu.VMEM((GROUP, 256, 256), F32),
            ],
        ),
        out_shape=jax.ShapeDtypeStruct((boxes, 8, 4096), BF16),
        compiler_params=pltpu.CompilerParams(vmem_limit_bytes=VMEM_LIMIT),
        cost_estimate=pl.CostEstimate(flops=10**9, bytes_accessed=27 * 10**6, transcendentals=0),
        name="box_apply",
    )(at, domains, pot, fine, jnp.asarray(np.ascontiguousarray(odd_x.T)), jnp.asarray(np.ascontiguousarray(wide.T)))


def permuted(rows, cols, a, back):
    at_row, at_col = (1, 0) if back else (0, 1)
    high = lax.Precision.HIGHEST
    a = lax.dot_general(rows[...], a, (((at_row,), (0,)), ((), ())), precision=high, preferred_element_type=F32)
    return lax.dot_general(a, cols[...], (((1,), (at_col,)), ((), ())), precision=high, preferred_element_type=F32)


def store_kernel(kxc, rows, cols, out):
    exact = permuted(rows, cols, kxc[...], False)
    out[0] = exact.astype(BF16)
    out[1] = (exact - out[0].astype(F32)).astype(BF16)


def natural_kernel(at_x, pot, rows, cols, out):
    out[...] = permuted(rows, cols, pot[at_x[0]].astype(F32), True).astype(BF16)


def small_call(kernel, scalars, arrays, shape, name):
    smem, vmem = pl.BlockSpec(memory_space=pltpu.SMEM), pl.BlockSpec(memory_space=pltpu.VMEM)
    return pl.pallas_call(
        kernel,
        in_specs=[smem] * len(scalars) + [vmem] * (len(arrays) + 2),
        out_specs=vmem,
        out_shape=jax.ShapeDtypeStruct(shape, BF16),
        cost_estimate=pl.CostEstimate(flops=10**7, bytes_accessed=10**6, transcendentals=0),
        name=name,
    )(*scalars, *arrays, *(jnp.asarray(o) for o in cell_orders()))


def shifted(array, axis, by):
    size = lax.axis_size(axis)
    return lax.ppermute(array, axis, [(i, (i + by) % size) for i in range(size)])


def on_device(functions, responses, box_domain, pair_index, pair_weight, kernel_xc):
    at_x, at_y, at_z = (lax.axis_index(a) for a in AXES)
    at = jnp.stack([at_y, at_z])
    domains = box_domain.reshape(-1)
    part, fine = box_density(at, domains, functions, responses, pair_index, pair_weight)
    kxc = small_call(store_kernel, (), (kernel_xc.reshape(64, 128),), (2, 64, 128), "kernel_order")

    part = part.reshape(3, 2, 4, 64, 128)
    lower = shifted(part[0], "gz", -1)
    upper = shifted(part[2], "gz", 1)
    by_z = (part[1].astype(F32) + lower.astype(F32) + upper.astype(F32)).astype(BF16)
    by_y = (by_z[1].astype(F32) + shifted(by_z[0], "gy", -1).astype(F32)).astype(BF16)
    sent = jnp.concatenate([by_y, kxc])
    got = [sent] + [shifted(sent, "gx", s) for s in (1, 2, 3)]
    total = sum(g[:4].astype(F32) for g in got)
    pot = []
    for x in range(4):
        which = (at_x - x) % 4
        high, low = (lax.select_n(which, *(g[k] for g in got)).astype(F32) for k in (4, 5))
        pot.append((total[x] * (high + low)).astype(BF16))
    pot = jnp.stack(pot)
    by_y = jnp.stack([shifted(pot, "gy", 1), pot])
    natural = small_call(natural_kernel, (at_x.reshape(1),), (pot,), (64, 128), "natural_order")
    by_z = jnp.stack([shifted(by_y, "gz", 1), by_y, shifted(by_y, "gz", -1)]).reshape(24, 64, 128)
    applied = box_apply(at, domains, by_z, fine)
    return applied, natural.reshape(1, 8192)


def solution(mesh):
    spec3, spec2 = P(AXES, None, None), P(AXES, None)
    return jax.shard_map(
        on_device,
        mesh=mesh,
        in_specs=(spec3, spec3, spec2, P(None, AXES, None), spec2, spec2),
        out_specs=(spec3, spec2),
        check_vma=False,
    )
```

```python
import jax
import jax.numpy as jnp
import ml_dtypes
import numpy as np
from jax import lax
from jax.experimental import pallas as pl
from jax.experimental.pallas import tpu as pltpu
from jax.sharding import PartitionSpec as P

AXES = ("gx", "gy", "gz")
GROUP = 16
LAG = 1
BF16 = jnp.bfloat16
F32 = jnp.float32


def tables():
    m = (2.0 * np.arange(64) + 1.0)[:, None]
    n = np.arange(64.0)[None, :]
    k = np.arange(1, 32)[:, None, None]
    total = 1.0 + 2.0 * np.cos(2.0 * np.pi * k * (m / 128 - n / 64)).sum(0)
    total = total + np.cos(np.pi * n) * np.cos(np.pi * m / 2)
    odd = (total / 64).astype(ml_dtypes.bfloat16)
    x_of = np.concatenate([np.arange(0, 64, 2), np.arange(1, 64, 2)])
    odd_x = odd[x_of][:, x_of]
    wide = np.zeros((256, 256), ml_dtypes.bfloat16)
    for i in range(4):
        wide[64 * i : 64 * i + 64, 64 * i : 64 * i + 64] = odd.T
    return odd_x, wide


def cell_orders():
    rows = np.zeros((64, 64), np.float32)
    for par in range(2):
        for p in range(2):
            for c in range(16):
                rows[4 * c + 2 * p + par, (par * 2 + p) * 16 + c] = 1
    cols = np.zeros((128, 128), np.float32)
    for par in range(2):
        for y in range(64):
            cols[par * 64 + y, 2 * y + par] = 1
    return rows, cols


def lane_low(shape):
    return lax.broadcasted_iota(jnp.int32, shape, len(shape) - 1) % 128 < 64


def slots_of(at, domain):
    box_x = lax.div(domain, 32)
    slot_y = lax.rem(lax.rem(lax.div(domain, 8), 4) - at[0] + 5, 4)
    slot_z = lax.rem(lax.rem(domain, 8) - at[1] + 9, 8)
    base = (slot_z * 2 + slot_y) * 4
    return base + box_x, base + lax.rem(box_x + 1, 4)


def in_turn(stages, lag=LAG):
    for t in range(GROUP + lag * (len(stages) - 1)):
        for i, stage in enumerate(stages):
            if 0 <= t - lag * i < GROUP:
                stage(t - lag * i)


def density_kernel(at, domains, func, resp, pidx, pw, spread, odd_x, wide, part0, part1, part2, fine, acc, stage, mixer, rs):
    step = pl.program_id(0)
    rows8 = 8 * GROUP

    @pl.when(step == 0)
    def _():
        acc[...] = jnp.zeros_like(acc)

        def widen(a, precision=None):
            return jnp.dot(a, spread[...], precision=precision, preferred_element_type=F32)

        level = (lax.broadcasted_iota(jnp.int32, (24, 640), 1) % 8).astype(F32)
        weight = widen(pw[...], lax.Precision.HIGHEST)
        first = jnp.where(widen(pidx[0].astype(F32)) == level, weight, 0.0)
        second = jnp.where(widen(pidx[1].astype(F32)) == level, 1.0, 0.0)
        at_row = lax.broadcasted_iota(jnp.int32, (128, 128), 0)
        at_col = lax.broadcasted_iota(jnp.int32, (128, 128), 1)
        cycle = jnp.where(at_row % 8 == at_col % 8, 1.0, 0.0).astype(BF16)
        for i in range(5):
            cut = slice(128 * i, 128 * i + 128)
            cross = lax.dot_general(
                first[:, cut],
                second[:, cut],
                (((0,), (0,)), ((), ())),
                precision=lax.Precision.HIGHEST,
                preferred_element_type=F32,
            )
            cross = jnp.where(at_row // 8 == at_col // 8, cross, 0.0).astype(BF16)
            mixer[cut] = jnp.dot(cross, cycle, preferred_element_type=F32)

    low = lane_low((32, 128))
    on_block = (
        lax.broadcasted_iota(jnp.int32, (16, 8, 128), 0) == lax.broadcasted_iota(jnp.int32, (16, 8, 128), 2) // 8
    )

    def place(which, b):
        return fine.at[b, 0] if which == 0 else rs.at[b]

    def mix(b):
        pairs = mixer[pl.ds(pl.multiple_of((step * GROUP + b) * 8, 8), 8), :]
        pairs = jnp.where(on_block, jnp.broadcast_to(pairs[None], (16, 8, 128)), 0.0)
        pairs = pairs.reshape(128, 128).astype(BF16)
        raw = jnp.concatenate([resp[b, :128], resp[b, 128:]], axis=1)
        mixed = jnp.dot(pairs, raw, preferred_element_type=F32)
        stage[0, b] = func[b].astype(F32)
        stage[1, b, :128] = mixed[:, :128]
        stage[1, b, 128:] = mixed[:, 128:]

    def regroup(b):
        for which in range(2):
            to = place(which, b)
            for h in range(4):
                one = stage[which, b, pl.ds(2 * h, 32, stride=8), :]
                two = stage[which, b, pl.ds(2 * h + 1, 32, stride=8), :]
                p0 = jnp.where(low, one, pltpu.roll(two, 64, 1)).astype(BF16)
                p1 = jnp.where(low, pltpu.roll(one, 64, 1), two).astype(BF16)
                row, lane = 128 * (h // 2), 128 * (h % 2)
                to[row : row + 32, lane : lane + 128] = p0
                to[row + 32 : row + 64, lane : lane + 128] = p1

    def along_x(b):
        for which in range(2):
            to = place(which, b)
            for i in range(2):
                even = to[128 * i : 128 * i + 64, :]
                odd = jnp.dot(odd_x[...], even, preferred_element_type=F32)
                to[128 * i + 64 : 128 * i + 128, :] = odd.astype(BF16)

    def along_y(b):
        tall_f = fine[b, 0]
        tall_r = rs[b]
        shift_f = jnp.dot(tall_f, wide[...], preferred_element_type=F32)
        shift_r = jnp.dot(tall_r, wide[...], preferred_element_type=F32)
        fine[b, 1] = shift_f.astype(BF16)
        den_e = tall_f.astype(F32) * tall_r.astype(F32)
        den_o = shift_f * shift_r
        s0, s1 = slots_of(at, domains[step * GROUP + b])
        for par, den in ((0, den_e), (1, den_o)):
            den = den[:128] + den[128:]
            den = den[:, :128] + den[:, 128:]
            for g in range(4):
                acc[s0, par, 16 * g : 16 * g + 16] += den[32 * g : 32 * g + 16]
                acc[s1, par, 16 * g : 16 * g + 16] += den[32 * g + 16 : 32 * g + 32]

    in_turn((mix, regroup, along_x, along_y))

    @pl.when(step == pl.num_programs(0) - 1)
    def _():
        lowd = lane_low((64, 128))

        def fold(d, _):
            sums = [acc[d, par] + pltpu.roll(acc[d, par], 64, 1) for par in range(2)]
            to = (part0, part1, part2)[d // 8]
            to[d % 8] = jnp.where(lowd, sums[0], sums[1]).astype(BF16)

        for d in range(24):
            fold(d, 0)


def as_tiles(array):
    boxes = array.shape[0]
    return array.reshape(boxes, 8, 32, 128).transpose(0, 2, 1, 3).reshape(boxes, 256, 128)


def box_density(at, domains, functions, responses, pair_index, pair_weight):
    boxes = functions.shape[0]
    odd_x, wide = tables()
    steps = boxes // GROUP
    spread = np.repeat(np.eye(boxes, dtype=np.float32), 8, axis=1)
    return pl.pallas_call(
        density_kernel,
        grid_spec=pltpu.PrefetchScalarGridSpec(
            num_scalar_prefetch=2,
            grid=(steps,),
            in_specs=[
                pl.BlockSpec((GROUP, 256, 128), lambda i, *_: (i, 0, 0)),
                pl.BlockSpec((GROUP, 256, 128), lambda i, *_: (i, 0, 0)),
                pl.BlockSpec((2, 24, boxes), lambda i, *_: (0, 0, 0)),
                pl.BlockSpec((24, boxes), lambda i, *_: (0, 0)),
                pl.BlockSpec((boxes, 8 * boxes), lambda i, *_: (0, 0)),
                pl.BlockSpec((64, 64), lambda i, *_: (0, 0)),
                pl.BlockSpec((256, 256), lambda i, *_: (0, 0)),
            ],
            out_specs=[
                *[pl.BlockSpec((8, 64, 128), lambda i, *_: (0, 0, 0))] * 3,
                pl.BlockSpec((GROUP, 2, 256, 256), lambda i, *_: (i, 0, 0, 0)),
            ],
            scratch_shapes=[
                pltpu.VMEM((24, 2, 64, 128), F32),
                pltpu.VMEM((2, GROUP, 256, 128), F32),
                pltpu.VMEM((8 * boxes, 128), F32),
                pltpu.VMEM((GROUP, 256, 256), BF16),
            ],
        ),
        out_shape=[
            *[jax.ShapeDtypeStruct((8, 64, 128), BF16)] * 3,
            jax.ShapeDtypeStruct((boxes, 2, 256, 256), BF16),
        ],
        compiler_params=pltpu.CompilerParams(vmem_limit_bytes=60 * 1024 * 1024),
        cost_estimate=pl.CostEstimate(flops=2 * 10**9, bytes_accessed=32 * 10**6, transcendentals=0),
        name="box_density",
    )(
        at,
        domains,
        as_tiles(functions),
        as_tiles(responses),
        jnp.transpose(pair_index, (0, 2, 1)),
        jnp.transpose(pair_weight, (1, 0)),
        jnp.asarray(spread),
        jnp.asarray(odd_x),
        jnp.asarray(wide),
    )


def apply_kernel(at, domains, pot, fine, odd_xt, wide_t, out, twice, stage, col):
    step = pl.program_id(0)

    @pl.when(step == 0)
    def _():
        lowd = lane_low((64, 128))

        def double(d, _):
            own = pot[d].astype(F32) * 0.25
            other = pltpu.roll(own, 64, 1)
            twice[d, 0] = jnp.where(lowd, own, other).astype(BF16)
            twice[d, 1] = jnp.where(lowd, other, own).astype(BF16)
            return 0

        for d in range(24):
            double(d, 0)

    low = lane_low((32, 128))
    def back_y(b):
        s0, s1 = slots_of(at, domains[step * GROUP + b])
        weighted = []
        for par in range(2):
            pieces = []
            for g in range(4):
                pieces.append(twice[s0, par, 16 * g : 16 * g + 16])
                pieces.append(twice[s1, par, 16 * g : 16 * g + 16])
            level = jnp.concatenate(pieces, axis=0)
            level = jnp.concatenate([level, level], axis=1)
            level = jnp.concatenate([level, level], axis=0)
            weighted.append(level * fine[b, par])
        col[b] = weighted[0].astype(F32) + jnp.dot(weighted[1], wide_t[...], preferred_element_type=F32)

    def back_x(b):
        for i in range(2):
            odd = col[b, 128 * i + 64 : 128 * i + 128].astype(BF16)
            res = col[b, 128 * i : 128 * i + 64] + jnp.dot(odd_xt[...], odd, preferred_element_type=F32)
            for k in range(2):
                p0 = res[:32, 128 * k : 128 * k + 128]
                p1 = res[32:, 128 * k : 128 * k + 128]
                f = 4 * i + 2 * k
                stage[b, pl.ds(f, 32, stride=8), :] = jnp.where(low, p0, pltpu.roll(p1, 64, 1))
                stage[b, pl.ds(f + 1, 32, stride=8), :] = jnp.where(low, pltpu.roll(p0, 64, 1), p1)

    def regroup(b):
        out[b] = stage[b].astype(BF16)

    in_turn((back_y, back_x, regroup), GROUP)


def box_apply(at, domains, pot, fine):
    boxes = fine.shape[0]
    odd_x, wide = tables()
    steps = boxes // GROUP
    out = pl.pallas_call(
        apply_kernel,
        grid_spec=pltpu.PrefetchScalarGridSpec(
            num_scalar_prefetch=2,
            grid=(steps,),
            in_specs=[
                pl.BlockSpec((24, 64, 128), lambda i, *_: (0, 0, 0)),
                pl.BlockSpec((GROUP, 2, 256, 256), lambda i, *_: (i, 0, 0, 0)),
                pl.BlockSpec((64, 64), lambda i, *_: (0, 0)),
                pl.BlockSpec((256, 256), lambda i, *_: (0, 0)),
            ],
            out_specs=pl.BlockSpec((GROUP, 256, 128), lambda i, *_: (i, 0, 0)),
            scratch_shapes=[
                pltpu.VMEM((24, 2, 64, 128), BF16),
                pltpu.VMEM((GROUP, 256, 128), F32),
                pltpu.VMEM((GROUP, 256, 256), F32),
            ],
        ),
        out_shape=jax.ShapeDtypeStruct((boxes, 256, 128), BF16),
        compiler_params=pltpu.CompilerParams(vmem_limit_bytes=60 * 1024 * 1024),
        cost_estimate=pl.CostEstimate(flops=10**9, bytes_accessed=27 * 10**6, transcendentals=0),
        name="box_apply",
    )(at, domains, pot, fine, jnp.asarray(np.ascontiguousarray(odd_x.T)), jnp.asarray(np.ascontiguousarray(wide.T)))
    return out.reshape(boxes, 32, 8, 128).transpose(0, 2, 1, 3).reshape(boxes, 8, 4096)


def permuted(rows, cols, a, back):
    at_row, at_col = (1, 0) if back else (0, 1)
    high = lax.Precision.HIGHEST
    a = lax.dot_general(rows[...], a, (((at_row,), (0,)), ((), ())), precision=high, preferred_element_type=F32)
    return lax.dot_general(a, cols[...], (((1,), (at_col,)), ((), ())), precision=high, preferred_element_type=F32)


def store_kernel(kxc, rows, cols, out):
    exact = permuted(rows, cols, kxc[...], False)
    out[0] = exact.astype(BF16)
    out[1] = (exact - out[0].astype(F32)).astype(BF16)


def natural_kernel(at_x, pot, rows, cols, out):
    out[...] = permuted(rows, cols, pot[at_x[0]].astype(F32), True).astype(BF16)


def potential_kernel(at_x, *refs):
    got, pot = refs[:4], refs[4]
    for s in range(4):
        x = lax.rem(at_x[0] - s + 4, 4)
        total = sum(g[x].astype(F32) for g in got)
        kernel = got[s][4].astype(F32) + got[s][5].astype(F32)
        pot[x] = (total * kernel).astype(BF16)


def small_call(kernel, scalars, arrays, shape, name):
    smem, vmem = pl.BlockSpec(memory_space=pltpu.SMEM), pl.BlockSpec(memory_space=pltpu.VMEM)
    return pl.pallas_call(
        kernel,
        in_specs=[smem] * len(scalars) + [vmem] * len(arrays),
        out_specs=vmem,
        out_shape=jax.ShapeDtypeStruct(shape, BF16),
        cost_estimate=pl.CostEstimate(flops=10**7, bytes_accessed=10**6, transcendentals=0),
        compiler_params=pltpu.CompilerParams(vmem_limit_bytes=4 * 1024 * 1024),
        name=name,
    )(*scalars, *arrays)


def shifted(array, axis, by):
    size = lax.axis_size(axis)
    return lax.ppermute(array, axis, [(i, (i + by) % size) for i in range(size)])


def on_device(functions, responses, box_domain, pair_index, pair_weight, kernel_xc):
    at_x, at_y, at_z = (lax.axis_index(a) for a in AXES)
    at = jnp.stack([at_y, at_z])
    domains = box_domain.reshape(-1)
    *parts, fine = box_density(at, domains, functions, responses, pair_index, pair_weight)
    orders = [jnp.asarray(o) for o in cell_orders()]
    kxc = small_call(store_kernel, (), (kernel_xc.reshape(64, 128), *orders), (2, 64, 128), "kernel_order")

    lower = shifted(parts[0], "gz", -1)
    upper = shifted(parts[2], "gz", 1)
    by_z = (parts[1].astype(F32) + lower.astype(F32) + upper.astype(F32)).astype(BF16)
    by_y = (by_z[4:].astype(F32) + shifted(by_z[:4], "gy", -1).astype(F32)).astype(BF16)
    sent = jnp.concatenate([by_y, kxc])
    got = [sent] + [shifted(sent, "gx", s) for s in (1, 2, 3)]
    pot = small_call(potential_kernel, (at_x.reshape(1),), got, (4, 64, 128), "potential")
    by_y = jnp.stack([shifted(pot, "gy", 1), pot])
    natural = small_call(natural_kernel, (at_x.reshape(1),), (pot, *orders), (64, 128), "natural_order")
    by_z = jnp.stack([shifted(by_y, "gz", 1), by_y, shifted(by_y, "gz", -1)]).reshape(24, 64, 128)
    applied = box_apply(at, domains, by_z, fine)
    return applied, natural.reshape(1, 8192)


def solution(mesh):
    spec3, spec2 = P(AXES, None, None), P(AXES, None)
    return jax.shard_map(
        on_device,
        mesh=mesh,
        in_specs=(spec3, spec3, spec2, P(None, AXES, None), spec2, spec2),
        out_specs=(spec3, spec2),
        check_vma=False,
    )
```

```python
import jax
import jax.numpy as jnp
import ml_dtypes
import numpy as np
from jax import lax
from jax.experimental import pallas as pl
from jax.experimental.pallas import tpu as pltpu
from jax.sharding import PartitionSpec as P

AXES = ("gx", "gy", "gz")
GROUP = 16
HELD = 8
SLOTS = 4
BF16 = jnp.bfloat16
F32 = jnp.float32


def tables():
    m = (2.0 * np.arange(64) + 1.0)[:, None]
    n = np.arange(64.0)[None, :]
    k = np.arange(1, 32)[:, None, None]
    total = 1.0 + 2.0 * np.cos(2.0 * np.pi * k * (m / 128 - n / 64)).sum(0)
    total = total + np.cos(np.pi * n) * np.cos(np.pi * m / 2)
    odd = (total / 64).astype(ml_dtypes.bfloat16)
    x_of = np.concatenate([np.arange(0, 64, 2), np.arange(1, 64, 2)])
    odd_x = odd[x_of][:, x_of]
    wide = np.zeros((256, 256), ml_dtypes.bfloat16)
    for i in range(4):
        wide[64 * i : 64 * i + 64, 64 * i : 64 * i + 64] = odd.T
    return odd_x, wide


def cell_orders():
    rows = np.zeros((64, 64), np.float32)
    for par in range(2):
        for p in range(2):
            for c in range(16):
                rows[4 * c + 2 * p + par, (par * 2 + p) * 16 + c] = 1
    cols = np.zeros((128, 128), np.float32)
    for par in range(2):
        for y in range(64):
            cols[par * 64 + y, 2 * y + par] = 1
    return rows, cols


def lane_low(shape):
    return lax.broadcasted_iota(jnp.int32, shape, len(shape) - 1) % 128 < 64


def slots_of(at, domain):
    box_x = lax.div(domain, 32)
    slot_y = lax.rem(lax.rem(lax.div(domain, 8), 4) - at[0] + 5, 4)
    slot_z = lax.rem(lax.rem(domain, 8) - at[1] + 9, 8)
    base = (slot_z * 2 + slot_y) * 4
    return base + box_x, base + lax.rem(box_x + 1, 4)


def in_turn(stages, boxes, lag=1):
    for t in range(boxes + lag * (len(stages) - 1)):
        for i, stage in enumerate(stages):
            if 0 <= t - lag * i < boxes:
                stage(t - lag * i)


def density_kernel(at_y, at_z, domains, func, resp, pidx, pw, spread, odd_x, wide, part0, part1, part2, fine, acc, stage, mixer, rs):
    step = pl.program_id(0)
    rows8 = 8 * GROUP

    @pl.when(step == 0)
    def _():
        acc[...] = jnp.zeros_like(acc)

        def widen(a, precision=None):
            return jnp.dot(a, spread[...], precision=precision, preferred_element_type=F32)

        level = (lax.broadcasted_iota(jnp.int32, (24, 640), 1) % 8).astype(F32)
        weight = widen(pw[...], lax.Precision.HIGHEST)
        first = jnp.where(widen(pidx[0].astype(F32)) == level, weight, 0.0)
        second = jnp.where(widen(pidx[1].astype(F32)) == level, 1.0, 0.0)
        at_row = lax.broadcasted_iota(jnp.int32, (128, 128), 0)
        at_col = lax.broadcasted_iota(jnp.int32, (128, 128), 1)
        cycle = jnp.where(at_row % 8 == at_col % 8, 1.0, 0.0).astype(BF16)
        for i in range(5):
            cut = slice(128 * i, 128 * i + 128)
            cross = lax.dot_general(
                first[:, cut],
                second[:, cut],
                (((0,), (0,)), ((), ())),
                precision=lax.Precision.HIGHEST,
                preferred_element_type=F32,
            )
            cross = jnp.where(at_row // 8 == at_col // 8, cross, 0.0).astype(BF16)
            mixer[cut] = jnp.dot(cross, cycle, preferred_element_type=F32)

    low = lane_low((32, 128))
    on_block = (
        lax.broadcasted_iota(jnp.int32, (16, 8, 128), 0) == lax.broadcasted_iota(jnp.int32, (16, 8, 128), 2) // 8
    )

    def place(which, b):
        return fine.at[b, 0] if which == 0 else rs.at[b]

    def mix(b):
        pairs = mixer[pl.ds(pl.multiple_of((step * GROUP + b) * 8, 8), 8), :]
        pairs = jnp.where(on_block, jnp.broadcast_to(pairs[None], (16, 8, 128)), 0.0)
        pairs = pairs.reshape(128, 128).astype(BF16)
        raw = jnp.concatenate([resp[b, :128], resp[b, 128:]], axis=1)
        mixed = jnp.dot(pairs, raw, preferred_element_type=F32)
        stage[0, b] = func[b].astype(F32)
        stage[1, b, :128] = mixed[:, :128]
        stage[1, b, 128:] = mixed[:, 128:]

    def regroup(b):
        for which in range(2):
            to = place(which, b)
            for h in range(4):
                one = stage[which, b, pl.ds(2 * h, 32, stride=8), :]
                two = stage[which, b, pl.ds(2 * h + 1, 32, stride=8), :]
                p0 = jnp.where(low, one, pltpu.roll(two, 64, 1)).astype(BF16)
                p1 = jnp.where(low, pltpu.roll(one, 64, 1), two).astype(BF16)
                row, lane = 128 * (h // 2), 128 * (h % 2)
                to[row : row + 32, lane : lane + 128] = p0
                to[row + 32 : row + 64, lane : lane + 128] = p1

    def along_x(b):
        for which in range(2):
            to = place(which, b)
            for i in range(2):
                even = to[128 * i : 128 * i + 64, :]
                odd = jnp.dot(odd_x[...], even, preferred_element_type=F32)
                to[128 * i + 64 : 128 * i + 128, :] = odd.astype(BF16)

    def along_y(b):
        tall_f = fine[b, 0]
        tall_r = rs[b]
        shift_f = jnp.dot(tall_f, wide[...], preferred_element_type=F32).astype(BF16)
        shift_r = jnp.dot(tall_r, wide[...], preferred_element_type=F32).astype(BF16)
        fine[b, 1] = shift_f
        s0, s1 = slots_of((at_y[0], at_z[0]), domains[step * GROUP + b])
        for par, den in ((0, tall_f * tall_r), (1, shift_f * shift_r)):
            den = den[:128] + den[128:]
            den = (den[:, :128] + den[:, 128:]).astype(F32)
            for g in range(4):
                acc[s0, par, 16 * g : 16 * g + 16] += den[32 * g : 32 * g + 16]
                acc[s1, par, 16 * g : 16 * g + 16] += den[32 * g + 16 : 32 * g + 32]

    in_turn((mix, regroup, along_x, along_y), GROUP)

    @pl.when(step == pl.num_programs(0) - 1)
    def _():
        lowd = lane_low((64, 128))

        def fold(d, _):
            sums = [acc[d, par] + pltpu.roll(acc[d, par], 64, 1) for par in range(2)]
            to = (part0, part1, part2)[d // 8]
            to[d % 8] = jnp.where(lowd, sums[0], sums[1]).astype(BF16)

        for d in range(24):
            fold(d, 0)


def as_tiles(array):
    boxes = array.shape[0]
    return array.reshape(boxes, 8, 32, 128).transpose(0, 2, 1, 3).reshape(boxes, 256, 128)


def box_density(at, domains, functions, responses, pair_index, pair_weight):
    boxes = functions.shape[0]
    odd_x, wide = tables()
    steps = boxes // GROUP
    spread = np.repeat(np.eye(boxes, dtype=np.float32), 8, axis=1)
    arrays = (
        as_tiles(functions),
        as_tiles(responses),
        jnp.transpose(pair_index, (0, 2, 1)),
        jnp.transpose(pair_weight, (1, 0)),
        jnp.asarray(spread),
        jnp.asarray(odd_x),
        jnp.asarray(wide),
    )
    return pl.pallas_call(
        density_kernel,
        grid_spec=pltpu.PrefetchScalarGridSpec(
            num_scalar_prefetch=3,
            grid=(steps,),
            in_specs=[
                pl.BlockSpec((GROUP, 256, 128), lambda i, *_: (i, 0, 0)),
                pl.BlockSpec((GROUP, 256, 128), lambda i, *_: (i, 0, 0)),
                pl.BlockSpec((2, 24, boxes), lambda i, *_: (0, 0, 0)),
                pl.BlockSpec((24, boxes), lambda i, *_: (0, 0)),
                pl.BlockSpec((boxes, 8 * boxes), lambda i, *_: (0, 0)),
                pl.BlockSpec((64, 64), lambda i, *_: (0, 0)),
                pl.BlockSpec((256, 256), lambda i, *_: (0, 0)),
            ],
            out_specs=[
                *[pl.BlockSpec((8, 64, 128), lambda i, *_: (0, 0, 0))] * 3,
                pl.BlockSpec((GROUP, 2, 256, 256), lambda i, *_: (i, 0, 0, 0)),
            ],
            scratch_shapes=[
                pltpu.VMEM((24, 2, 64, 128), F32),
                pltpu.VMEM((2, GROUP, 256, 128), F32),
                pltpu.VMEM((8 * boxes, 128), F32),
                pltpu.VMEM((GROUP, 256, 256), BF16),
            ],
        ),
        out_shape=[
            *[jax.ShapeDtypeStruct((8, 64, 128), BF16)] * 3,
            jax.ShapeDtypeStruct((boxes, 2, 256, 256), BF16),
        ],
        compiler_params=pltpu.CompilerParams(vmem_limit_bytes=44 * 1024 * 1024),
        cost_estimate=pl.CostEstimate(flops=2 * 10**9, bytes_accessed=32 * 10**6, transcendentals=0),
        name="box_density",
    )(
        *at,
        domains,
        *(pltpu.with_memory_space_constraint(array, pltpu.HBM) for array in arrays),
    )


def apply_kernel(at_y, at_z, domains, pot0, pot1, pot2, fine, odd_xt, wide_t, out, twice, stage, col, held, sems):
    step = pl.program_id(0)
    steps = pl.num_programs(0) - 1

    def fetch(i):
        slot = lax.rem(i, SLOTS)
        return pltpu.make_async_copy(fine.at[pl.ds(i * HELD, HELD)], held.at[slot], sems.at[slot])

    @pl.when(step == 0)
    def _():
        for i in range(SLOTS - 1):
            fetch(i).start()

    @pl.when(step + SLOTS - 1 < steps)
    def _():
        fetch(step + SLOTS - 1).start()


    @pl.when(step == 0)
    def _():
        lowd = lane_low((64, 128))

        def double(d, _):
            own = (pot0, pot1, pot2)[d // 8][d % 8].astype(F32) * 0.25
            other = pltpu.roll(own, 64, 1)
            twice[d, 0] = jnp.where(lowd, own, other).astype(BF16)
            twice[d, 1] = jnp.where(lowd, other, own).astype(BF16)
            return 0

        for d in range(24):
            double(d, 0)

    @pl.when(step < steps)
    def _():
        fetch(step).wait()

    low = lane_low((32, 128))
    now = lax.rem(step, SLOTS)
    ahead = jnp.minimum(step, steps - 1) * HELD

    def back_y(b):
        s0, s1 = slots_of((at_y[0], at_z[0]), domains[ahead + b])
        weighted = []
        for par in range(2):
            pieces = []
            for g in range(4):
                pieces.append(twice[s0, par, 16 * g : 16 * g + 16])
                pieces.append(twice[s1, par, 16 * g : 16 * g + 16])
            level = jnp.concatenate(pieces, axis=0)
            level = jnp.concatenate([level, level], axis=1)
            level = jnp.concatenate([level, level], axis=0)
            weighted.append(level * held[now, b, par])
        col[b] = weighted[0].astype(F32) + jnp.dot(weighted[1], wide_t[...], preferred_element_type=F32)

    def back_x(b):
        for i in range(2):
            odd = col[b, 128 * i + 64 : 128 * i + 128].astype(BF16)
            res = col[b, 128 * i : 128 * i + 64] + jnp.dot(odd_xt[...], odd, preferred_element_type=F32)
            for k in range(2):
                p0 = res[:32, 128 * k : 128 * k + 128]
                p1 = res[32:, 128 * k : 128 * k + 128]
                f = 4 * i + 2 * k
                stage[b, pl.ds(f, 32, stride=8), :] = jnp.where(low, p0, pltpu.roll(p1, 64, 1))
                stage[b, pl.ds(f + 1, 32, stride=8), :] = jnp.where(low, pltpu.roll(p0, 64, 1), p1)

    def regroup(b):
        out[b] = stage[b].astype(BF16)

    in_turn((back_x, regroup, back_y), HELD)


def box_apply(at, domains, pots, fine):
    boxes = fine.shape[0]
    fine = pltpu.with_memory_space_constraint(fine, pltpu.HBM)
    odd_x, wide = tables()
    steps = boxes // HELD
    out = pl.pallas_call(
        apply_kernel,
        grid_spec=pltpu.PrefetchScalarGridSpec(
            num_scalar_prefetch=3,
            grid=(steps + 1,),
            in_specs=[
                *[pl.BlockSpec((8, 64, 128), lambda i, *_: (0, 0, 0))] * 3,
                pl.BlockSpec(memory_space=pl.ANY),
                pl.BlockSpec((64, 64), lambda i, *_: (0, 0)),
                pl.BlockSpec((256, 256), lambda i, *_: (0, 0)),
            ],
            out_specs=pl.BlockSpec((HELD, 256, 128), lambda i, *_: (jnp.maximum(i - 1, 0), 0, 0)),
            scratch_shapes=[
                pltpu.VMEM((24, 2, 64, 128), BF16),
                pltpu.VMEM((HELD, 256, 128), F32),
                pltpu.VMEM((HELD, 256, 256), F32),
                pltpu.VMEM((SLOTS, HELD, 2, 256, 256), BF16),
                pltpu.SemaphoreType.DMA((SLOTS,)),
            ],
        ),
        out_shape=jax.ShapeDtypeStruct((boxes, 256, 128), BF16),
        compiler_params=pltpu.CompilerParams(vmem_limit_bytes=44 * 1024 * 1024),
        cost_estimate=pl.CostEstimate(flops=10**9, bytes_accessed=27 * 10**6, transcendentals=0),
        name="box_apply",
    )(*at, domains, *pots, fine, jnp.asarray(np.ascontiguousarray(odd_x.T)), jnp.asarray(np.ascontiguousarray(wide.T)))
    return out.reshape(boxes, 32, 8, 128).transpose(0, 2, 1, 3).reshape(boxes, 8, 4096)


def permuted(rows, cols, a, back):
    at_row, at_col = (1, 0) if back else (0, 1)
    high = lax.Precision.HIGHEST
    a = lax.dot_general(rows[...], a, (((at_row,), (0,)), ((), ())), precision=high, preferred_element_type=F32)
    return lax.dot_general(a, cols[...], (((1,), (at_col,)), ((), ())), precision=high, preferred_element_type=F32)


def store_kernel(kxc, rows, cols, out):
    exact = permuted(rows, cols, kxc[...], False)
    out[0] = exact.astype(BF16)


def natural_kernel(at_x, pot, rows, cols, out):
    out[...] = permuted(rows, cols, pot[at_x[0]].astype(F32), True).astype(BF16)


def potential_kernel(at_x, *refs):
    got, pot = refs[:4], refs[4]
    for s in range(4):
        x = lax.rem(at_x[0] - s + 4, 4)
        total = sum(g[x].astype(F32) for g in got)
        kernel = got[s][4].astype(F32)
        pot[x] = (total * kernel).astype(BF16)


def small_call(kernel, scalars, arrays, shape, name):
    smem, vmem = pl.BlockSpec(memory_space=pltpu.SMEM), pl.BlockSpec(memory_space=pltpu.VMEM)
    return pl.pallas_call(
        kernel,
        in_specs=[smem] * len(scalars) + [vmem] * len(arrays),
        out_specs=vmem,
        out_shape=jax.ShapeDtypeStruct(shape, BF16),
        cost_estimate=pl.CostEstimate(flops=10**7, bytes_accessed=10**6, transcendentals=0),
        compiler_params=pltpu.CompilerParams(vmem_limit_bytes=4 * 1024 * 1024),
        name=name,
    )(*scalars, *arrays)


def shifted(array, axis, by):
    size = lax.axis_size(axis)
    return lax.ppermute(array, axis, [(i, (i + by) % size) for i in range(size)])


def on_device(functions, responses, box_domain, pair_index, pair_weight, kernel_xc):
    at_x, at_y, at_z = (lax.axis_index(a) for a in AXES)
    at = (at_y.reshape(1), at_z.reshape(1))
    domains = pltpu.with_memory_space_constraint(box_domain.reshape(-1), pltpu.HBM)
    *parts, fine = box_density(at, domains, functions, responses, pair_index, pair_weight)
    orders = [jnp.asarray(o) for o in cell_orders()]
    kxc = small_call(store_kernel, (), (kernel_xc.reshape(64, 128), *orders), (1, 64, 128), "kernel_order")

    lower = shifted(parts[0], "gz", -1)
    upper = shifted(parts[2], "gz", 1)
    by_z = (parts[1].astype(F32) + lower.astype(F32) + upper.astype(F32)).astype(BF16)
    by_y = (by_z[4:].astype(F32) + shifted(by_z[:4], "gy", -1).astype(F32)).astype(BF16)
    sent = jnp.concatenate([by_y, kxc])
    got = [sent] + [shifted(sent, "gx", s) for s in (1, 2, 3)]
    pot = small_call(potential_kernel, (at_x.reshape(1),), got, (4, 64, 128), "potential")
    by_y = jnp.concatenate([shifted(pot, "gy", 1), pot])
    natural = small_call(natural_kernel, (at_x.reshape(1),), (pot, *orders), (64, 128), "natural_order")
    by_z = (shifted(by_y, "gz", 1), by_y, shifted(by_y, "gz", -1))
    applied = box_apply(at, domains, by_z, fine)
    return applied, natural.reshape(1, 8192)


def solution(mesh):
    spec3, spec2 = P(AXES, None, None), P(AXES, None)
    return jax.shard_map(
        on_device,
        mesh=mesh,
        in_specs=(spec3, spec3, spec2, P(None, AXES, None), spec2, spec2),
        out_specs=(spec3, spec2),
        check_vma=False,
    )
```

```python
import jax
import jax.numpy as jnp
import ml_dtypes
import numpy as np
from jax import lax
from jax.experimental import pallas as pl
from jax.experimental.pallas import tpu as pltpu
from jax.sharding import PartitionSpec as P

AXES = ("gx", "gy", "gz")
GROUP = 20
HELD = 10
SENT = 4
SLOTS = 4
BF16 = jnp.bfloat16
F32 = jnp.float32


def tables():
    m = (2.0 * np.arange(64) + 1.0)[:, None]
    n = np.arange(64.0)[None, :]
    k = np.arange(1, 32)[:, None, None]
    total = 1.0 + 2.0 * np.cos(2.0 * np.pi * k * (m / 128 - n / 64)).sum(0)
    total = total + np.cos(np.pi * n) * np.cos(np.pi * m / 2)
    odd = (total / 64).astype(ml_dtypes.bfloat16)
    x_of = np.concatenate([np.arange(0, 64, 2), np.arange(1, 64, 2)])
    odd_x = odd[x_of][:, x_of]
    wide = np.zeros((256, 256), ml_dtypes.bfloat16)
    for i in range(4):
        wide[64 * i : 64 * i + 64, 64 * i : 64 * i + 64] = odd.T
    return odd_x, wide


def cell_orders():
    rows = np.zeros((64, 64), np.float32)
    for par in range(2):
        for p in range(2):
            for c in range(16):
                rows[4 * c + 2 * p + par, (par * 2 + p) * 16 + c] = 1
    cols = np.zeros((128, 128), np.float32)
    for par in range(2):
        for y in range(64):
            cols[par * 64 + y, 2 * y + par] = 1
    return rows, cols


def lane_low(shape):
    return lax.broadcasted_iota(jnp.int32, shape, len(shape) - 1) % 128 < 64


def slots_of(at, domain):
    box_x = lax.div(domain, 32)
    slot_y = lax.rem(lax.rem(lax.div(domain, 8), 4) - at[0] + 5, 4)
    slot_z = lax.rem(lax.rem(domain, 8) - at[1] + 9, 8)
    base = (slot_z * 2 + slot_y) * 4
    return base + box_x, base + lax.rem(box_x + 1, 4)


def in_turn(stages, boxes, lag=1):
    for t in range(boxes + lag * (len(stages) - 1)):
        for i, stage in enumerate(stages):
            if 0 <= t - lag * i < boxes:
                stage(t - lag * i)


def density_kernel(at_y, at_z, domains, func, resp, pidx, pw, spread, odd_x, wide, part0, part1, part2, fine, acc, stage, mixer, rs, held, sems):
    step = pl.program_id(0)
    parity = lax.rem(step, 2)

    def send(i, b):
        slot = lax.rem(i, 2)
        there = fine.at[pl.ds(i * GROUP + b, SENT)]
        return pltpu.make_async_copy(held.at[slot, pl.ds(b, SENT)], there, sems.at[slot, b // SENT])

    @pl.when(step >= 2)
    def _():
        for b in range(0, GROUP, SENT):
            send(step - 2, b).wait()

    rows8 = 8 * GROUP

    @pl.when(step == 0)
    def _():
        acc[...] = jnp.zeros_like(acc)

        def widen(a, precision=None):
            return jnp.dot(a, spread[...], precision=precision, preferred_element_type=F32)

        level = (lax.broadcasted_iota(jnp.int32, (24, 640), 1) % 8).astype(F32)
        weight = widen(pw[...], lax.Precision.HIGHEST)
        first = jnp.where(widen(pidx[0].astype(F32)) == level, weight, 0.0)
        second = jnp.where(widen(pidx[1].astype(F32)) == level, 1.0, 0.0)
        at_row = lax.broadcasted_iota(jnp.int32, (128, 128), 0)
        at_col = lax.broadcasted_iota(jnp.int32, (128, 128), 1)
        cycle = jnp.where(at_row % 8 == at_col % 8, 1.0, 0.0).astype(BF16)
        for i in range(5):
            cut = slice(128 * i, 128 * i + 128)
            cross = lax.dot_general(
                first[:, cut],
                second[:, cut],
                (((0,), (0,)), ((), ())),
                precision=lax.Precision.HIGHEST,
                preferred_element_type=F32,
            )
            cross = jnp.where(at_row // 8 == at_col // 8, cross, 0.0).astype(BF16)
            mixer[cut] = jnp.dot(cross, cycle, preferred_element_type=F32)

    low = lane_low((32, 128))
    on_block = (
        lax.broadcasted_iota(jnp.int32, (16, 8, 128), 0) == lax.broadcasted_iota(jnp.int32, (16, 8, 128), 2) // 8
    )

    def place(which, b):
        return held.at[parity, b, 0] if which == 0 else rs.at[b]

    def mix(b):
        pairs = mixer[pl.ds(pl.multiple_of((step * GROUP + b) * 8, 8), 8), :]
        pairs = jnp.where(on_block, jnp.broadcast_to(pairs[None], (16, 8, 128)), 0.0)
        pairs = pairs.reshape(128, 128).astype(BF16)
        raw = jnp.concatenate([resp[b, :128], resp[b, 128:]], axis=1)
        mixed = jnp.dot(pairs, raw, preferred_element_type=F32)
        stage[0, b] = func[b].astype(F32)
        stage[1, b, :128] = mixed[:, :128]
        stage[1, b, 128:] = mixed[:, 128:]

    def regroup(b):
        for which in range(2):
            to = place(which, b)
            for h in range(4):
                one = stage[which, b, pl.ds(2 * h, 32, stride=8), :]
                two = stage[which, b, pl.ds(2 * h + 1, 32, stride=8), :]
                p0 = jnp.where(low, one, pltpu.roll(two, 64, 1)).astype(BF16)
                p1 = jnp.where(low, pltpu.roll(one, 64, 1), two).astype(BF16)
                row, lane = 128 * (h // 2), 128 * (h % 2)
                to[row : row + 32, lane : lane + 128] = p0
                to[row + 32 : row + 64, lane : lane + 128] = p1

    def along_x(b):
        for which in range(2):
            to = place(which, b)
            for i in range(2):
                even = to[128 * i : 128 * i + 64, :]
                odd = jnp.dot(odd_x[...], even, preferred_element_type=F32)
                to[128 * i + 64 : 128 * i + 128, :] = odd.astype(BF16)

    def along_y(b):
        tall_f = held[parity, b, 0]
        tall_r = rs[b]
        shift_f = jnp.dot(tall_f, wide[...], preferred_element_type=F32).astype(BF16)
        shift_r = jnp.dot(tall_r, wide[...], preferred_element_type=F32).astype(BF16)
        held[parity, b, 1] = shift_f
        if b % SENT == SENT - 1:
            send(step, b + 1 - SENT).start()
        s0, s1 = slots_of((at_y[0], at_z[0]), domains[step * GROUP + b])
        for par, den in ((0, tall_f * tall_r), (1, shift_f * shift_r)):
            den = den[:128] + den[128:]
            den = (den[:, :128] + den[:, 128:]).astype(F32)
            for g in range(4):
                acc[s0, par, 16 * g : 16 * g + 16] += den[32 * g : 32 * g + 16]
                acc[s1, par, 16 * g : 16 * g + 16] += den[32 * g + 16 : 32 * g + 32]

    in_turn((mix, regroup, along_x, along_y), GROUP)

    @pl.when(step == pl.num_programs(0) - 1)
    def _():
        lowd = lane_low((64, 128))

        def fold(d, _):
            sums = [acc[d, par] + pltpu.roll(acc[d, par], 64, 1) for par in range(2)]
            to = (part0, part1, part2)[d // 8]
            to[d % 8] = jnp.where(lowd, sums[0], sums[1]).astype(BF16)

        for d in range(24):
            fold(d, 0)
        for i in (step - 1, step):
            for b in range(0, GROUP, SENT):
                send(i, b).wait()


def as_tiles(array):
    boxes = array.shape[0]
    return array.reshape(boxes, 8, 32, 128).transpose(0, 2, 1, 3).reshape(boxes, 256, 128)


def box_density(at, domains, functions, responses, pair_index, pair_weight):
    boxes = functions.shape[0]
    odd_x, wide = tables()
    steps = boxes // GROUP
    spread = np.repeat(np.eye(boxes, dtype=np.float32), 8, axis=1)
    arrays = (
        as_tiles(functions),
        as_tiles(responses),
        jnp.transpose(pair_index, (0, 2, 1)),
        jnp.transpose(pair_weight, (1, 0)),
        jnp.asarray(spread),
        jnp.asarray(odd_x),
        jnp.asarray(wide),
    )
    return pl.pallas_call(
        density_kernel,
        grid_spec=pltpu.PrefetchScalarGridSpec(
            num_scalar_prefetch=3,
            grid=(steps,),
            in_specs=[
                pl.BlockSpec((GROUP, 256, 128), lambda i, *_: (i, 0, 0)),
                pl.BlockSpec((GROUP, 256, 128), lambda i, *_: (i, 0, 0)),
                pl.BlockSpec((2, 24, boxes), lambda i, *_: (0, 0, 0)),
                pl.BlockSpec((24, boxes), lambda i, *_: (0, 0)),
                pl.BlockSpec((boxes, 8 * boxes), lambda i, *_: (0, 0)),
                pl.BlockSpec((64, 64), lambda i, *_: (0, 0)),
                pl.BlockSpec((256, 256), lambda i, *_: (0, 0)),
            ],
            out_specs=[
                *[pl.BlockSpec((8, 64, 128), lambda i, *_: (0, 0, 0))] * 3,
                pl.BlockSpec(memory_space=pl.ANY),
            ],
            scratch_shapes=[
                pltpu.VMEM((24, 2, 64, 128), F32),
                pltpu.VMEM((2, GROUP, 256, 128), F32),
                pltpu.VMEM((8 * boxes, 128), F32),
                pltpu.VMEM((GROUP, 256, 256), BF16),
                pltpu.VMEM((2, GROUP, 2, 256, 256), BF16),
                pltpu.SemaphoreType.DMA((2, GROUP // SENT)),
            ],
        ),
        out_shape=[
            *[jax.ShapeDtypeStruct((8, 64, 128), BF16)] * 3,
            jax.ShapeDtypeStruct((boxes, 2, 256, 256), BF16),
        ],
        compiler_params=pltpu.CompilerParams(vmem_limit_bytes=44 * 1024 * 1024),
        cost_estimate=pl.CostEstimate(flops=2 * 10**9, bytes_accessed=32 * 10**6, transcendentals=0),
        name="box_density",
    )(
        *at,
        domains,
        *(pltpu.with_memory_space_constraint(array, pltpu.HBM) for array in arrays),
    )


def apply_kernel(at_y, at_z, domains, pot0, pot1, pot2, fine, odd_xt, wide_t, out, twice, stage, col, held, sems):
    step = pl.program_id(0)
    steps = pl.num_programs(0) - 1

    def fetch(i):
        slot = lax.rem(i, SLOTS)
        return pltpu.make_async_copy(fine.at[pl.ds(i * HELD, HELD)], held.at[slot], sems.at[slot])

    @pl.when(step == 0)
    def _():
        for i in range(SLOTS - 1):
            fetch(i).start()

    @pl.when(step + SLOTS - 1 < steps)
    def _():
        fetch(step + SLOTS - 1).start()


    @pl.when(step == 0)
    def _():
        lowd = lane_low((64, 128))

        def double(d, _):
            own = (pot0, pot1, pot2)[d // 8][d % 8].astype(F32) * 0.25
            other = pltpu.roll(own, 64, 1)
            twice[d, 0] = jnp.where(lowd, own, other).astype(BF16)
            twice[d, 1] = jnp.where(lowd, other, own).astype(BF16)
            return 0

        for d in range(24):
            double(d, 0)

    @pl.when(step < steps)
    def _():
        fetch(step).wait()

    low = lane_low((32, 128))
    now = lax.rem(step, SLOTS)
    ahead = jnp.minimum(step, steps - 1) * HELD

    def back_y(b):
        s0, s1 = slots_of((at_y[0], at_z[0]), domains[ahead + b])
        weighted = []
        for par in range(2):
            pieces = []
            for g in range(4):
                pieces.append(twice[s0, par, 16 * g : 16 * g + 16])
                pieces.append(twice[s1, par, 16 * g : 16 * g + 16])
            level = jnp.concatenate(pieces, axis=0)
            level = jnp.concatenate([level, level], axis=1)
            level = jnp.concatenate([level, level], axis=0)
            weighted.append(level * held[now, b, par])
        col[b] = weighted[0].astype(F32) + jnp.dot(weighted[1], wide_t[...], preferred_element_type=F32)

    def back_x(b):
        for i in range(2):
            odd = col[b, 128 * i + 64 : 128 * i + 128].astype(BF16)
            res = col[b, 128 * i : 128 * i + 64] + jnp.dot(odd_xt[...], odd, preferred_element_type=F32)
            for k in range(2):
                p0 = res[:32, 128 * k : 128 * k + 128]
                p1 = res[32:, 128 * k : 128 * k + 128]
                f = 4 * i + 2 * k
                stage[b, pl.ds(f, 32, stride=8), :] = jnp.where(low, p0, pltpu.roll(p1, 64, 1))
                stage[b, pl.ds(f + 1, 32, stride=8), :] = jnp.where(low, pltpu.roll(p0, 64, 1), p1)

    def regroup(b):
        out[b] = stage[b].astype(BF16)

    in_turn((back_x, regroup, back_y), HELD)


def box_apply(at, domains, pots, fine):
    boxes = fine.shape[0]
    fine = pltpu.with_memory_space_constraint(fine, pltpu.HBM)
    odd_x, wide = tables()
    steps = boxes // HELD
    out = pl.pallas_call(
        apply_kernel,
        grid_spec=pltpu.PrefetchScalarGridSpec(
            num_scalar_prefetch=3,
            grid=(steps + 1,),
            in_specs=[
                *[pl.BlockSpec((8, 64, 128), lambda i, *_: (0, 0, 0))] * 3,
                pl.BlockSpec(memory_space=pl.ANY),
                pl.BlockSpec((64, 64), lambda i, *_: (0, 0)),
                pl.BlockSpec((256, 256), lambda i, *_: (0, 0)),
            ],
            out_specs=pl.BlockSpec((HELD, 256, 128), lambda i, *_: (jnp.maximum(i - 1, 0), 0, 0)),
            scratch_shapes=[
                pltpu.VMEM((24, 2, 64, 128), BF16),
                pltpu.VMEM((HELD, 256, 128), F32),
                pltpu.VMEM((HELD, 256, 256), F32),
                pltpu.VMEM((SLOTS, HELD, 2, 256, 256), BF16),
                pltpu.SemaphoreType.DMA((SLOTS,)),
            ],
        ),
        out_shape=jax.ShapeDtypeStruct((boxes, 256, 128), BF16),
        compiler_params=pltpu.CompilerParams(vmem_limit_bytes=44 * 1024 * 1024),
        cost_estimate=pl.CostEstimate(flops=10**9, bytes_accessed=27 * 10**6, transcendentals=0),
        name="box_apply",
    )(*at, domains, *pots, fine, jnp.asarray(np.ascontiguousarray(odd_x.T)), jnp.asarray(np.ascontiguousarray(wide.T)))
    return out.reshape(boxes, 32, 8, 128).transpose(0, 2, 1, 3).reshape(boxes, 8, 4096)


def permuted(rows, cols, a, back):
    at_row, at_col = (1, 0) if back else (0, 1)
    high = lax.Precision.HIGHEST
    a = lax.dot_general(rows[...], a, (((at_row,), (0,)), ((), ())), precision=high, preferred_element_type=F32)
    return lax.dot_general(a, cols[...], (((1,), (at_col,)), ((), ())), precision=high, preferred_element_type=F32)


def store_kernel(kxc, rows, cols, out):
    exact = permuted(rows, cols, kxc[...], False)
    out[0] = exact.astype(BF16)


def natural_kernel(at_x, pot, rows, cols, out):
    out[...] = permuted(rows, cols, pot[at_x[0]].astype(F32), True).astype(BF16)


def potential_kernel(at_x, *refs):
    got, pot = refs[:4], refs[4]
    for s in range(4):
        x = lax.rem(at_x[0] - s + 4, 4)
        total = sum(g[x].astype(F32) for g in got)
        kernel = got[s][4].astype(F32)
        pot[x] = (total * kernel).astype(BF16)


def small_call(kernel, scalars, arrays, shape, name):
    smem, vmem = pl.BlockSpec(memory_space=pltpu.SMEM), pl.BlockSpec(memory_space=pltpu.VMEM)
    return pl.pallas_call(
        kernel,
        in_specs=[smem] * len(scalars) + [vmem] * len(arrays),
        out_specs=vmem,
        out_shape=jax.ShapeDtypeStruct(shape, BF16),
        cost_estimate=pl.CostEstimate(flops=10**7, bytes_accessed=10**6, transcendentals=0),
        compiler_params=pltpu.CompilerParams(vmem_limit_bytes=4 * 1024 * 1024),
        name=name,
    )(*scalars, *arrays)


def shifted(array, axis, by):
    size = lax.axis_size(axis)
    return lax.ppermute(array, axis, [(i, (i + by) % size) for i in range(size)])


def on_device(functions, responses, box_domain, pair_index, pair_weight, kernel_xc):
    at_x, at_y, at_z = (lax.axis_index(a) for a in AXES)
    at = (at_y.reshape(1), at_z.reshape(1))
    domains = pltpu.with_memory_space_constraint(box_domain.reshape(-1), pltpu.HBM)
    *parts, fine = box_density(at, domains, functions, responses, pair_index, pair_weight)
    orders = [jnp.asarray(o) for o in cell_orders()]
    kxc = small_call(store_kernel, (), (kernel_xc.reshape(64, 128), *orders), (1, 64, 128), "kernel_order")

    lower = shifted(parts[0], "gz", -1)
    upper = shifted(parts[2], "gz", 1)
    by_z = (parts[1].astype(F32) + lower.astype(F32) + upper.astype(F32)).astype(BF16)
    by_y = (by_z[4:].astype(F32) + shifted(by_z[:4], "gy", -1).astype(F32)).astype(BF16)
    sent = jnp.concatenate([by_y, kxc])
    got = [sent] + [shifted(sent, "gx", s) for s in (1, 2, 3)]
    pot = small_call(potential_kernel, (at_x.reshape(1),), got, (4, 64, 128), "potential")
    by_y = jnp.concatenate([shifted(pot, "gy", 1), pot])
    natural = small_call(natural_kernel, (at_x.reshape(1),), (pot, *orders), (64, 128), "natural_order")
    by_z = (shifted(by_y, "gz", 1), by_y, shifted(by_y, "gz", -1))
    applied = box_apply(at, domains, by_z, fine)
    return applied, natural.reshape(1, 8192)


def solution(mesh):
    spec3, spec2 = P(AXES, None, None), P(AXES, None)
    return jax.shard_map(
        on_device,
        mesh=mesh,
        in_specs=(spec3, spec3, spec2, P(None, AXES, None), spec2, spec2),
        out_specs=(spec3, spec2),
        check_vma=False,
    )
```

```python
import jax
import jax.numpy as jnp
import ml_dtypes
import numpy as np
from jax import lax
from jax.experimental import pallas as pl
from jax.experimental.pallas import tpu as pltpu
from jax.sharding import PartitionSpec as P

AXES = ("gx", "gy", "gz")
GROUP = 20
HELD = 10
SENT = 4
SLOTS = 4
BF16 = jnp.bfloat16
F32 = jnp.float32


def tables():
    m = (2.0 * np.arange(64) + 1.0)[:, None]
    n = np.arange(64.0)[None, :]
    k = np.arange(1, 32)[:, None, None]
    total = 1.0 + 2.0 * np.cos(2.0 * np.pi * k * (m / 128 - n / 64)).sum(0)
    total = total + np.cos(np.pi * n) * np.cos(np.pi * m / 2)
    odd = (total / 64).astype(ml_dtypes.bfloat16)
    x_of = np.concatenate([np.arange(0, 64, 2), np.arange(1, 64, 2)])
    odd_x = odd[x_of][:, x_of]
    wide = np.zeros((256, 256), ml_dtypes.bfloat16)
    for i in range(4):
        wide[64 * i : 64 * i + 64, 64 * i : 64 * i + 64] = odd.T
    return odd_x, wide


def cell_orders():
    rows = np.zeros((64, 64), np.float32)
    for par in range(2):
        for p in range(2):
            for c in range(16):
                rows[4 * c + 2 * p + par, (par * 2 + p) * 16 + c] = 1
    cols = np.zeros((128, 128), np.float32)
    for par in range(2):
        for y in range(64):
            cols[par * 64 + y, 2 * y + par] = 1
    return rows, cols


def lane_low(shape):
    return lax.broadcasted_iota(jnp.int32, shape, len(shape) - 1) % 128 < 64


def slots_of(at, domain):
    box_x = lax.div(domain, 32)
    slot_y = lax.rem(lax.rem(lax.div(domain, 8), 4) - at[0] + 5, 4)
    slot_z = lax.rem(lax.rem(domain, 8) - at[1] + 9, 8)
    base = (slot_z * 2 + slot_y) * 4
    return base + box_x, base + lax.rem(box_x + 1, 4)


def in_turn(stages, boxes, lag=1):
    for t in range(boxes + lag * (len(stages) - 1)):
        for i, stage in enumerate(stages):
            if 0 <= t - lag * i < boxes:
                stage(t - lag * i)


def density_kernel(at_y, at_z, domains, func, resp, pidx, pw, spread, odd_x, wide, part0, part1, part2, fine, acc, stage, mixer, rs, held, sems):
    step = pl.program_id(0)
    parity = lax.rem(step, 2)

    def send(i, b):
        slot = lax.rem(i, 2)
        there = fine.at[pl.ds(i * GROUP + b, SENT)]
        return pltpu.make_async_copy(held.at[slot, pl.ds(b, SENT)], there, sems.at[slot, b // SENT])

    @pl.when(step >= 2)
    def _():
        for b in range(0, GROUP, SENT):
            send(step - 2, b).wait()

    rows8 = 8 * GROUP

    @pl.when(step == 0)
    def _():
        acc[...] = jnp.zeros_like(acc)

        def widen(a):
            return jnp.dot(a.astype(BF16), spread[...], preferred_element_type=F32)

        level = (lax.broadcasted_iota(jnp.int32, (24, 640), 1) % 8).astype(F32)
        weight = widen(pw[...])
        first = jnp.where(widen(pidx[0].astype(F32)) == level, weight, 0.0)
        second = jnp.where(widen(pidx[1].astype(F32)) == level, 1.0, 0.0)
        at_row = lax.broadcasted_iota(jnp.int32, (128, 128), 0)
        at_col = lax.broadcasted_iota(jnp.int32, (128, 128), 1)
        cycle = jnp.where(at_row % 8 == at_col % 8, 1.0, 0.0).astype(BF16)
        for i in range(5):
            cut = slice(128 * i, 128 * i + 128)
            cross = lax.dot_general(
                first[:, cut].astype(BF16),
                second[:, cut].astype(BF16),
                (((0,), (0,)), ((), ())),
                preferred_element_type=F32,
            )
            cross = jnp.where(at_row // 8 == at_col // 8, cross, 0.0).astype(BF16)
            mixer[cut] = jnp.dot(cross, cycle, preferred_element_type=F32)

    low = lane_low((32, 128))
    on_block = (
        lax.broadcasted_iota(jnp.int32, (16, 8, 128), 0) == lax.broadcasted_iota(jnp.int32, (16, 8, 128), 2) // 8
    )

    def place(which, b):
        return held.at[parity, b, 0] if which == 0 else rs.at[b]

    def mix(b):
        pairs = mixer[pl.ds(pl.multiple_of((step * GROUP + b) * 8, 8), 8), :]
        pairs = jnp.where(on_block, jnp.broadcast_to(pairs[None], (16, 8, 128)), 0.0)
        pairs = pairs.reshape(128, 128).astype(BF16)
        raw = jnp.concatenate([resp[b, :128], resp[b, 128:]], axis=1)
        mixed = jnp.dot(pairs, raw, preferred_element_type=F32)
        stage[0, b] = func[b].astype(F32)
        stage[1, b, :128] = mixed[:, :128]
        stage[1, b, 128:] = mixed[:, 128:]

    def regroup(b):
        for which in range(2):
            to = place(which, b)
            for h in range(4):
                one = stage[which, b, pl.ds(2 * h, 32, stride=8), :]
                two = stage[which, b, pl.ds(2 * h + 1, 32, stride=8), :]
                p0 = jnp.where(low, one, pltpu.roll(two, 64, 1)).astype(BF16)
                p1 = jnp.where(low, pltpu.roll(one, 64, 1), two).astype(BF16)
                row, lane = 128 * (h // 2), 128 * (h % 2)
                to[row : row + 32, lane : lane + 128] = p0
                to[row + 32 : row + 64, lane : lane + 128] = p1

    def along_x(b):
        for which in range(2):
            to = place(which, b)
            for i in range(2):
                even = to[128 * i : 128 * i + 64, :]
                odd = jnp.dot(odd_x[...], even, preferred_element_type=F32)
                to[128 * i + 64 : 128 * i + 128, :] = odd.astype(BF16)

    def along_y(b):
        tall_f = held[parity, b, 0]
        tall_r = rs[b]
        shift_f = jnp.dot(tall_f, wide[...], preferred_element_type=F32).astype(BF16)
        shift_r = jnp.dot(tall_r, wide[...], preferred_element_type=F32).astype(BF16)
        held[parity, b, 1] = shift_f
        if b % SENT == SENT - 1:
            send(step, b + 1 - SENT).start()
        s0, s1 = slots_of((at_y[0], at_z[0]), domains[step * GROUP + b])
        for par, den in ((0, tall_f * tall_r), (1, shift_f * shift_r)):
            den = den[:128] + den[128:]
            den = (den[:, :128] + den[:, 128:]).astype(F32)
            for g in range(4):
                acc[s0, par, 16 * g : 16 * g + 16] += den[32 * g : 32 * g + 16]
                acc[s1, par, 16 * g : 16 * g + 16] += den[32 * g + 16 : 32 * g + 32]

    in_turn((mix, regroup, along_x, along_y), GROUP)

    @pl.when(step == pl.num_programs(0) - 1)
    def _():
        lowd = lane_low((64, 128))

        def fold(d, _):
            sums = [acc[d, par] + pltpu.roll(acc[d, par], 64, 1) for par in range(2)]
            to = (part0, part1, part2)[d // 8]
            to[d % 8] = jnp.where(lowd, sums[0], sums[1]).astype(BF16)

        for d in range(24):
            fold(d, 0)
        for i in (step - 1, step):
            for b in range(0, GROUP, SENT):
                send(i, b).wait()


def as_tiles(array):
    boxes = array.shape[0]
    return array.reshape(boxes, 8, 32, 128).transpose(0, 2, 1, 3).reshape(boxes, 256, 128)


def box_density(at, domains, functions, responses, pair_index, pair_weight):
    boxes = functions.shape[0]
    odd_x, wide = tables()
    steps = boxes // GROUP
    spread = np.repeat(np.eye(boxes), 8, axis=1).astype(ml_dtypes.bfloat16)
    arrays = (
        as_tiles(functions),
        as_tiles(responses),
        jnp.transpose(pair_index, (0, 2, 1)),
        jnp.transpose(pair_weight, (1, 0)),
        jnp.asarray(spread),
        jnp.asarray(odd_x),
        jnp.asarray(wide),
    )
    return pl.pallas_call(
        density_kernel,
        grid_spec=pltpu.PrefetchScalarGridSpec(
            num_scalar_prefetch=3,
            grid=(steps,),
            in_specs=[
                pl.BlockSpec((GROUP, 256, 128), lambda i, *_: (i, 0, 0)),
                pl.BlockSpec((GROUP, 256, 128), lambda i, *_: (i, 0, 0)),
                pl.BlockSpec((2, 24, boxes), lambda i, *_: (0, 0, 0)),
                pl.BlockSpec((24, boxes), lambda i, *_: (0, 0)),
                pl.BlockSpec((boxes, 8 * boxes), lambda i, *_: (0, 0)),
                pl.BlockSpec((64, 64), lambda i, *_: (0, 0)),
                pl.BlockSpec((256, 256), lambda i, *_: (0, 0)),
            ],
            out_specs=[
                *[pl.BlockSpec((8, 64, 128), lambda i, *_: (0, 0, 0))] * 3,
                pl.BlockSpec(memory_space=pl.ANY),
            ],
            scratch_shapes=[
                pltpu.VMEM((24, 2, 64, 128), F32),
                pltpu.VMEM((2, GROUP, 256, 128), F32),
                pltpu.VMEM((8 * boxes, 128), F32),
                pltpu.VMEM((GROUP, 256, 256), BF16),
                pltpu.VMEM((2, GROUP, 2, 256, 256), BF16),
                pltpu.SemaphoreType.DMA((2, GROUP // SENT)),
            ],
        ),
        out_shape=[
            *[jax.ShapeDtypeStruct((8, 64, 128), BF16)] * 3,
            jax.ShapeDtypeStruct((boxes, 2, 256, 256), BF16),
        ],
        compiler_params=pltpu.CompilerParams(vmem_limit_bytes=44 * 1024 * 1024),
        cost_estimate=pl.CostEstimate(flops=2 * 10**9, bytes_accessed=32 * 10**6, transcendentals=0),
        name="box_density",
    )(
        *at,
        domains,
        *(pltpu.with_memory_space_constraint(array, pltpu.HBM) for array in arrays),
    )


def apply_kernel(at_y, at_z, domains, pot0, pot1, pot2, fine, odd_xt, wide_t, out, twice, stage, col, held, sems):
    step = pl.program_id(0)
    steps = pl.num_programs(0) - 1

    def fetch(i):
        slot = lax.rem(i, SLOTS)
        return pltpu.make_async_copy(fine.at[pl.ds(i * HELD, HELD)], held.at[slot], sems.at[slot])

    @pl.when(step == 0)
    def _():
        for i in range(SLOTS - 1):
            fetch(i).start()

    @pl.when(step + SLOTS - 1 < steps)
    def _():
        fetch(step + SLOTS - 1).start()


    @pl.when(step == 0)
    def _():
        lowd = lane_low((64, 128))

        def double(d, _):
            own = (pot0, pot1, pot2)[d // 8][d % 8].astype(F32) * 0.25
            other = pltpu.roll(own, 64, 1)
            twice[d, 0] = jnp.where(lowd, own, other).astype(BF16)
            twice[d, 1] = jnp.where(lowd, other, own).astype(BF16)
            return 0

        for d in range(24):
            double(d, 0)

    @pl.when(step < steps)
    def _():
        fetch(step).wait()

    low = lane_low((32, 128))
    now = lax.rem(step, SLOTS)
    ahead = jnp.minimum(step, steps - 1) * HELD

    def back_y(b):
        s0, s1 = slots_of((at_y[0], at_z[0]), domains[ahead + b])
        weighted = []
        for par in range(2):
            pieces = []
            for g in range(4):
                pieces.append(twice[s0, par, 16 * g : 16 * g + 16])
                pieces.append(twice[s1, par, 16 * g : 16 * g + 16])
            level = jnp.concatenate(pieces, axis=0)
            level = jnp.concatenate([level, level], axis=1)
            level = jnp.concatenate([level, level], axis=0)
            weighted.append(level * held[now, b, par])
        col[b] = weighted[0].astype(F32) + jnp.dot(weighted[1], wide_t[...], preferred_element_type=F32)

    def back_x(b):
        for i in range(2):
            odd = col[b, 128 * i + 64 : 128 * i + 128].astype(BF16)
            res = col[b, 128 * i : 128 * i + 64] + jnp.dot(odd_xt[...], odd, preferred_element_type=F32)
            for k in range(2):
                p0 = res[:32, 128 * k : 128 * k + 128]
                p1 = res[32:, 128 * k : 128 * k + 128]
                f = 4 * i + 2 * k
                stage[b, pl.ds(f, 32, stride=8), :] = jnp.where(low, p0, pltpu.roll(p1, 64, 1))
                stage[b, pl.ds(f + 1, 32, stride=8), :] = jnp.where(low, pltpu.roll(p0, 64, 1), p1)

    def regroup(b):
        out[b] = stage[b].astype(BF16)

    in_turn((back_x, regroup, back_y), HELD)


def box_apply(at, domains, pots, fine):
    boxes = fine.shape[0]
    fine = pltpu.with_memory_space_constraint(fine, pltpu.HBM)
    odd_x, wide = tables()
    steps = boxes // HELD
    out = pl.pallas_call(
        apply_kernel,
        grid_spec=pltpu.PrefetchScalarGridSpec(
            num_scalar_prefetch=3,
            grid=(steps + 1,),
            in_specs=[
                *[pl.BlockSpec((8, 64, 128), lambda i, *_: (0, 0, 0))] * 3,
                pl.BlockSpec(memory_space=pl.ANY),
                pl.BlockSpec((64, 64), lambda i, *_: (0, 0)),
                pl.BlockSpec((256, 256), lambda i, *_: (0, 0)),
            ],
            out_specs=pl.BlockSpec((HELD, 256, 128), lambda i, *_: (jnp.maximum(i - 1, 0), 0, 0)),
            scratch_shapes=[
                pltpu.VMEM((24, 2, 64, 128), BF16),
                pltpu.VMEM((HELD, 256, 128), F32),
                pltpu.VMEM((HELD, 256, 256), F32),
                pltpu.VMEM((SLOTS, HELD, 2, 256, 256), BF16),
                pltpu.SemaphoreType.DMA((SLOTS,)),
            ],
        ),
        out_shape=jax.ShapeDtypeStruct((boxes, 256, 128), BF16),
        compiler_params=pltpu.CompilerParams(vmem_limit_bytes=44 * 1024 * 1024),
        cost_estimate=pl.CostEstimate(flops=10**9, bytes_accessed=27 * 10**6, transcendentals=0),
        name="box_apply",
    )(*at, domains, *pots, fine, jnp.asarray(np.ascontiguousarray(odd_x.T)), jnp.asarray(np.ascontiguousarray(wide.T)))
    return out.reshape(boxes, 32, 8, 128).transpose(0, 2, 1, 3).reshape(boxes, 8, 4096)


def permuted(rows, cols, a, back):
    at_row, at_col = (1, 0) if back else (0, 1)
    high = lax.Precision.HIGHEST
    a = lax.dot_general(rows[...], a, (((at_row,), (0,)), ((), ())), precision=high, preferred_element_type=F32)
    return lax.dot_general(a, cols[...], (((1,), (at_col,)), ((), ())), precision=high, preferred_element_type=F32)


def store_kernel(kxc, rows, cols, out):
    exact = permuted(rows, cols, kxc[...], False)
    out[0] = exact.astype(BF16)


def natural_kernel(at_x, pot, rows, cols, out):
    out[...] = permuted(rows, cols, pot[at_x[0]].astype(F32), True).astype(BF16)


def potential_kernel(at_x, *refs):
    got, pot = refs[:4], refs[4]
    for s in range(4):
        x = lax.rem(at_x[0] - s + 4, 4)
        total = sum(g[x].astype(F32) for g in got)
        kernel = got[s][4].astype(F32)
        pot[x] = (total * kernel).astype(BF16)


def small_call(kernel, scalars, arrays, shape, name):
    smem, vmem = pl.BlockSpec(memory_space=pltpu.SMEM), pl.BlockSpec(memory_space=pltpu.VMEM)
    return pl.pallas_call(
        kernel,
        in_specs=[smem] * len(scalars) + [vmem] * len(arrays),
        out_specs=vmem,
        out_shape=jax.ShapeDtypeStruct(shape, BF16),
        cost_estimate=pl.CostEstimate(flops=10**7, bytes_accessed=10**6, transcendentals=0),
        compiler_params=pltpu.CompilerParams(vmem_limit_bytes=4 * 1024 * 1024),
        name=name,
    )(*scalars, *arrays)


def shifted(array, axis, by):
    size = lax.axis_size(axis)
    return lax.ppermute(array, axis, [(i, (i + by) % size) for i in range(size)])


def on_device(functions, responses, box_domain, pair_index, pair_weight, kernel_xc):
    at_x, at_y, at_z = (lax.axis_index(a) for a in AXES)
    at = (at_y.reshape(1), at_z.reshape(1))
    domains = pltpu.with_memory_space_constraint(box_domain.reshape(-1), pltpu.HBM)
    *parts, fine = box_density(at, domains, functions, responses, pair_index, pair_weight)
    orders = [jnp.asarray(o) for o in cell_orders()]
    kxc = small_call(store_kernel, (), (kernel_xc.reshape(64, 128), *orders), (1, 64, 128), "kernel_order")

    lower = shifted(parts[0], "gz", -1)
    upper = shifted(parts[2], "gz", 1)
    by_z = (parts[1].astype(F32) + lower.astype(F32) + upper.astype(F32)).astype(BF16)
    by_y = (by_z[4:].astype(F32) + shifted(by_z[:4], "gy", -1).astype(F32)).astype(BF16)
    sent = jnp.concatenate([by_y, kxc])
    got = [sent] + [shifted(sent, "gx", s) for s in (1, 2, 3)]
    pot = small_call(potential_kernel, (at_x.reshape(1),), got, (4, 64, 128), "potential")
    by_y = jnp.concatenate([shifted(pot, "gy", 1), pot])
    natural = small_call(natural_kernel, (at_x.reshape(1),), (pot, *orders), (64, 128), "natural_order")
    by_z = (shifted(by_y, "gz", 1), by_y, shifted(by_y, "gz", -1))
    applied = box_apply(at, domains, by_z, fine)
    return applied, natural.reshape(1, 8192)


def solution(mesh):
    spec3, spec2 = P(AXES, None, None), P(AXES, None)
    return jax.shard_map(
        on_device,
        mesh=mesh,
        in_specs=(spec3, spec3, spec2, P(None, AXES, None), spec2, spec2),
        out_specs=(spec3, spec2),
        check_vma=False,
    )
```
